256 devices in a mesh: ctx: 32 (over z_hi, x, core), head: 8 (over z_lo, y).
Axes of the slice: x: 4, y: 4, z: 8 (z_hi: 4, z_lo: 2; z = z_hi * 2 + z_lo), core: 2. Of those that a mesh axis runs over, the one named last changes fastest.
Arguments:
- block_order: int32 [32], replicated, may hold values from 0 to 31, each once
- queries: bfloat16 [4096, 4096], P('ctx', 'head'), may hold values from -36 to 36
- latent: bfloat16 [4096, 512], P('ctx'), may hold values from -6 to 6
- rope_keys: bfloat16 [4096, 128], P('ctx'), may hold values from -12 to 12
- w_uk: bfloat16 [512, 3584], P(None, 'head'), may hold values from -0.25 to 0.25
- w_uv: bfloat16 [512, 4096], P(None, 'head'), may hold values from -0.25 to 0.25
- cotangent: bfloat16 [4096, 4096], P('ctx', 'head'), may hold values from -6 to 6
- attn_out: bfloat16 [4096, 4096], P('ctx', 'head'), may hold values from -6 to 6
Outputs:
- d_queries: bfloat16 [4096, 4096], P('ctx', 'head')
- d_latent: float32 [4096, 512], P('ctx')
- d_rope_keys: float32 [4096, 128], P('ctx')
- d_w_uk: float32 [512, 3584], P('ctx', 'head')
The draws below stay inside these ranges and needn't reach their ends.
Inputs may be any that keep to these rules, and one draw needn't show every extreme that they name: A permutation of the blocks; index i of ctx holds the positions block_order[i] * 128 to block_order[i] * 128 + 127 of the window.
All inputs are finite; a program needn't handle non-finite values.
Results may differ from the reference program's by a relative error of at most 0.0075.
Values may be sent and summed in bfloat16 or wider, within the bound.
A program may use at most 128 MiB of HBM per device.

```python
import math
import jax
import jax.numpy as jnp
from jax import lax

TOK_DEV = 128
H = 32
KVG = 8
NOPE = 112
ROPE = 16
VD = 128
R = 512
TOKENS = 4096
BLOCKS = 32


def draw_queries(key, part):
    key = jax.random.fold_in(key, 5)
    base_key = jax.random.fold_in(key, 0)
    base = jnp.clip(jax.random.normal(base_key, (TOKENS, H, NOPE + ROPE)), -6.0, 6.0)
    return base.reshape(TOKENS, H * (NOPE + ROPE)).astype(jnp.bfloat16)


def draw_rope_keys(key, part):
    key = jax.random.fold_in(key, 9)
    base = jnp.clip(jax.random.normal(key, (TOKENS, KVG, ROPE)), -6.0, 6.0)
    return base.reshape(TOKENS, KVG * ROPE).astype(jnp.bfloat16)


def shard_levels(key, extent, cuts, smallest, top_value):
    level = 1.0
    for position, blocks in cuts:
        steps = jax.random.uniform(jax.random.fold_in(jax.random.fold_in(key, 6), position), (blocks,), jnp.float32, smallest / len(cuts), top_value / len(cuts))
        level = level * jnp.repeat(jnp.exp(steps), extent[position] // blocks).reshape((-1,) + (1,) * (len(extent) - 1 - position))
    return level


def scatter_about(rng, extent, deviation, bound, cuts=(), kind=jnp.bfloat16):
    values = jax.random.normal(rng, extent, jnp.float32) * deviation
    if len(cuts) > 0:
        values = shard_levels(rng, extent, cuts, -0.22, 0.18) * values
    return jnp.clip(values, min=-bound, max=bound).astype(kind)


def setup_inputs(seed: int = 0) -> dict:
    keys = jax.random.split(jax.random.key(seed), 9)
    return {
        "block_order": jax.random.permutation(keys[0], BLOCKS).astype(jnp.int32),
        "queries": draw_queries(jax.random.fold_in(keys[8], 71), 0),
        "latent": scatter_about(keys[2], (TOKENS, R), 1.0, 6.0, ((0, 32),)),
        "rope_keys": draw_rope_keys(jax.random.fold_in(keys[8], 71), 0),
        "w_uk": scatter_about(keys[4], (R, H * NOPE), R ** -0.5, 0.25, ((1, 8),)),
        "w_uv": scatter_about(keys[5], (R, H * VD), R ** -0.5, 0.25, ((1, 8),)),
        "cotangent": scatter_about(keys[6], (TOKENS, H * VD), 1.0, 6.0, ((0, 32), (1, 8))),
        "attn_out": scatter_about(keys[7], (TOKENS, H * VD), 1.0, 6.0, ((0, 32), (1, 8))),
    }


def reference(block_order, queries, latent, rope_keys, w_uk, w_uv, cotangent, attn_out):
    head_width = NOPE + ROPE
    scale_factor = 1.0 / math.sqrt(head_width)
    row_ids = jnp.arange(TOKENS, dtype=jnp.int32)
    positions = block_order[row_ids // TOK_DEV] * TOK_DEV + row_ids % TOK_DEV
    allowed = positions[None, :] <= positions[:, None]
    per_group = H // KVG

    def one_head(carry, head):
        lat_grad, rope_grad = carry
        q_head = lax.dynamic_slice_in_dim(queries, (head * head_width).astype(jnp.int32), head_width, 1)
        q_nope = q_head[:, :NOPE]
        q_rope = q_head[:, NOPE:]
        uk_head = lax.dynamic_slice_in_dim(w_uk, (head * NOPE).astype(jnp.int32), NOPE, 1)
        uv_head = lax.dynamic_slice_in_dim(w_uv, (head * VD).astype(jnp.int32), VD, 1)
        cot_head = lax.dynamic_slice_in_dim(cotangent, (head * VD).astype(jnp.int32), VD, 1)
        out_head = lax.dynamic_slice_in_dim(attn_out, (head * VD).astype(jnp.int32), VD, 1)
        group_start = (head // per_group * ROPE).astype(jnp.int32)
        rope_head = lax.dynamic_slice_in_dim(rope_keys, group_start, ROPE, 1)
        q_lat = jnp.dot(q_nope, uk_head.T, preferred_element_type=jnp.float32).astype(jnp.bfloat16)
        scores = (jnp.dot(q_lat, latent.T, preferred_element_type=jnp.float32) + jnp.dot(q_rope, rope_head.T, preferred_element_type=jnp.float32)) * scale_factor
        scores = jnp.where(allowed, scores, jnp.float32(-1e+30))
        row_max = lax.optimization_barrier(jnp.max(scores, axis=1, keepdims=True))
        log_total = row_max + jnp.log(lax.optimization_barrier(jnp.sum(jnp.exp(scores - row_max), axis=1, keepdims=True)))
        weights = jnp.exp(scores - log_total)
        probs = weights.astype(jnp.bfloat16)
        out_lat = jnp.dot(cot_head, uv_head.T, preferred_element_type=jnp.float32).astype(jnp.bfloat16)
        delta = lax.optimization_barrier(jnp.sum(cot_head.astype(jnp.float32) * out_head.astype(jnp.float32), axis=1, keepdims=True))
        dots = jnp.dot(out_lat, latent.T, preferred_element_type=jnp.float32)
        grad_scores = (weights * (dots - delta) * scale_factor).astype(jnp.bfloat16)
        dq_lat = jnp.dot(grad_scores, latent, preferred_element_type=jnp.float32).astype(jnp.bfloat16)
        dq_nope = jnp.dot(dq_lat, uk_head, preferred_element_type=jnp.float32)
        dq_rope = jnp.dot(grad_scores, rope_head, preferred_element_type=jnp.float32)
        dq_head = jnp.concatenate([dq_nope, dq_rope], axis=1).astype(jnp.bfloat16)
        dwuk_head = jnp.dot(dq_lat.T, q_nope, preferred_element_type=jnp.float32)
        lat_grad = lat_grad + jnp.dot(grad_scores.T, q_lat, preferred_element_type=jnp.float32) + jnp.dot(probs.T, out_lat, preferred_element_type=jnp.float32)
        rope_part = jnp.dot(grad_scores.T, q_rope, preferred_element_type=jnp.float32)
        previous = lax.dynamic_slice_in_dim(rope_grad, group_start, ROPE, 1)
        rope_grad = lax.dynamic_update_slice_in_dim(rope_grad, previous + rope_part, group_start, 1)
        return ((lat_grad, rope_grad), (dq_head, dwuk_head))
    initial = (jnp.zeros((TOKENS, R), jnp.float32), jnp.zeros((TOKENS, KVG * ROPE), jnp.float32))
    (lat_grad, rope_grad), (dq_all, dwuk_all) = lax.scan(one_head, initial, jnp.arange(H, dtype=jnp.int32))
    d_queries = jnp.transpose(dq_all, (1, 0, 2)).reshape(TOKENS, H * head_width)
    d_w_uk = jnp.transpose(dwuk_all, (1, 0, 2)).reshape(R, H * NOPE)
    return (d_queries, lat_grad, rope_grad, d_w_uk)
```

```python
import math

import jax
import jax.numpy as jnp
from jax import lax
from jax.experimental import pallas as pl
from jax.experimental.pallas import tpu as pltpu
from jax.sharding import PartitionSpec as P

KVG = 8
NOPE = 112
ROPE = 16
HD = 128
TOK = 128
LH = 4
R = 512
AUG = 640
NQ = 4
NK = 8
ROWS = LH * TOK
KEYS = NK * TOK
F32 = jnp.float32
BF16 = jnp.bfloat16
NEG = -1e30
SCALE = 1.0 / math.sqrt(HD)
LOG2E = math.log2(math.e)
MESH = pl.DeviceIdType.MESH

Q_R, Q_L, Q_F, C_R, C_L, C_F, D_R, D_L, D_O = range(9)
LAT_Z, ROPE_Z, LAT_C, ROPE_C = 9, 12, 15, 19
STAT = 23
DL_C, DL_Y, DL_Z, DL_G = 26, 27, 30, 38
DQ_X = 46
DW_C, DW_X, DW_Z = 49, 50, 53
DR_C, DR_Z, DR_G = 56, 57, 60
N_COPY = 68


def nt(a, b):
    return lax.dot_general(a, b, (((1,), (1,)), ((), ())), preferred_element_type=F32)


def nn(a, b):
    return jnp.dot(a, b, preferred_element_type=F32)


def iota(shape, dim):
    return lax.broadcasted_iota(jnp.int32, shape, dim)


def kernel(
    bo, q_in, lat_in, rope_in, wuk, wuv, cot_in, att_in,
    dq_out, dlat_out, drope_out, dw_out,
    q_all, c_all, delta, kaug, kr, rope_t, lat_t, waug, waug_t,
    qa_t, q_lat, o_lat_t, o_lat, s_t, dots_t, gs_t, pr_t,
    lse, lse_r, m_loc,
    dl_own, dl_send, dl_rcv, y_f, y_send, y_rcv, z_f, z_send, z_rcv, ag,
    dqa, dq_send, dq_own, dq_rcv,
    dw_acc, dw_f, dw_send, dw_c, dw_xf, dw_xs, dw_xr, dw_zf, dw_zs, dw_zr,
    dr_send, dr_c, dr_f, dr_z, dr_g,
    ssem, rsem,
):
    ctx = lax.axis_index("ctx")
    head = lax.axis_index("head")
    c, x, zh = ctx % 2, (ctx // 2) % 4, ctx // 8
    y, zl = head % 4, head // 4
    z = zh * 2 + zl

    def dev(zz, xx, yy, cc):
        zz, xx, yy = zz % 8, xx % 4, yy % 4
        return (((zz // 2) * 4 + xx) * 2 + cc, (zz % 2) * 4 + yy)

    sib = dev(z, x, y, 1 - c)

    def copy(src, dst, sid, rid, target):
        return pltpu.make_async_remote_copy(
            src_ref=src, dst_ref=dst, send_sem=ssem.at[sid], recv_sem=rsem.at[rid],
            device_id=target, device_id_type=MESH,
        )

    barrier = pltpu.get_barrier_semaphore()
    peers = [sib]
    peers += [dev(z, x + d, y, c) for d in range(1, 4)]
    peers += [dev(z + d, x, y, c) for d in range(1, 8)]
    peers += [dev(z, x, y + d, c) for d in range(1, 4)]
    peers += [dev(zh * 2 + 1 - zl, x, y + d, c) for d in range(1, 4)]
    for p in peers:
        pl.semaphore_signal(barrier, inc=1, device_id=p, device_id_type=MESH)

    rope_t[...] = jnp.transpose(rope_in[...].astype(F32)).astype(BF16)
    ones = jnp.ones((8, HD), BF16)
    for h in range(LH):
        cols = slice(h * HD, (h + 1) * HD)
        prod = cot_in[:, cols].astype(F32) * att_in[:, cols].astype(F32)
        high = prod.astype(BF16)
        low = (prod - high.astype(F32)).astype(BF16)
        delta[0, :, h * TOK:(h + 1) * TOK] = nt(ones, high) + nt(ones, low)
    q_all[0] = q_in[...]
    c_all[0] = cot_in[...]
    kr[0] = rope_t[pl.ds(pl.multiple_of(head * ROPE, ROPE), ROPE), :]
    pl.semaphore_wait(barrier, len(peers))

    right, left, far = dev(z, x + 1, y, c), dev(z, x + 3, y, c), dev(z, x + 2, y, c)
    s = 2 * zl - 1
    near = 3 - 2 * zl
    z_to = [dev(z + s + 8, x, y, c), dev(z + 2 * s + 8, x, y, c), dev(z + 3 * s + 8, x, y, c)]
    z_slot = [near, near, 2]
    other = 1 - zl
    z_group = [other * 4 + y, head, other * 4 + y]
    rope_own = [rope_t.at[pl.ds(pl.multiple_of(g * ROPE, ROPE), ROPE), :] for g in z_group]
    lat_dst = lambda slot: kaug.at[slot, :, pl.ds(0, R)]
    lat_z = [copy(lat_in, lat_dst(z_slot[i]), LAT_Z + i, LAT_Z + z_slot[i] - 1, z_to[i]) for i in range(3)]
    rope_z = [copy(rope_own[i], kr.at[z_slot[i]], ROPE_Z + i, ROPE_Z + z_slot[i] - 1, z_to[i]) for i in range(3)]
    lat_own = copy(lat_in, lat_dst(4), LAT_C, LAT_C, sib)
    kr_own = copy(kr.at[0], kr.at[4], ROPE_C, ROPE_C, sib)
    q_r = copy(q_in, q_all.at[1], Q_R, Q_R, right)
    q_l = copy(q_in, q_all.at[3], Q_L, Q_L, left)
    c_r = copy(cot_in, c_all.at[1], C_R, C_R, right)
    c_l = copy(cot_in, c_all.at[3], C_L, C_L, left)
    d_r = copy(delta.at[0], delta.at[1], D_R, D_R, right)
    d_l = copy(delta.at[0], delta.at[3], D_L, D_L, left)
    d_o = copy(delta.at[0], delta.at[2], D_O, D_O, far)
    q_f = copy(q_all.at[1], q_all.at[2], Q_F, Q_F, right)
    c_f = copy(c_all.at[3], c_all.at[2], C_F, C_F, left)
    first = [q_r, c_l, q_l, c_r, lat_z[0], lat_z[1], lat_z[2], lat_own, kr_own] + rope_z + [d_r, d_l, d_o]
    for op in first:
        op.start()

    ei, ej = iota((LH * NOPE, LH * HD), 0), iota((LH * NOPE, LH * HD), 1)
    spread = ((ei == (ej // HD) * NOPE + ej % HD) & (ej % HD < NOPE)).astype(F32).astype(BF16)
    waug[0:R, :] = nn(wuk[...], spread).astype(BF16)
    si, sj = iota((AUG - R, LH * HD), 0), iota((AUG - R, LH * HD), 1)
    waug[R:AUG, :] = (si == sj % HD - NOPE).astype(F32).astype(BF16)
    fi, fj = iota((LH * HD, LH * NOPE), 0), iota((LH * HD, LH * NOPE), 1)
    spread_t = ((fj == (fi // HD) * NOPE + fi % HD) & (fi % HD < NOPE)).astype(F32).astype(BF16)
    waug_t[:, 0:R] = nt(spread_t, wuk[...]).astype(BF16)
    ti, tj = iota((LH * HD, AUG - R), 0), iota((LH * HD, AUG - R), 1)
    waug_t[:, R:AUG] = (tj == ti % HD - NOPE).astype(F32).astype(BF16)
    kaug[0, :, 0:R] = lat_in[...]

    def project(slot):
        for h in range(LH):
            cols = slice(h * HD, (h + 1) * HD)
            rows = slice(h * TOK, (h + 1) * TOK)
            qh = q_all[slot, :, cols]
            ch = c_all[slot, :, cols]
            qa_t[slot, :, rows] = nt(waug[:, cols], qh).astype(BF16)
            q_lat[slot, rows, :] = nt(qh, waug[0:R, cols]).astype(BF16)
            o_lat_t[slot, :, rows] = nt(wuv[:, cols], ch).astype(BF16)
            o_lat[slot, rows, :] = nt(ch, wuv[:, cols]).astype(BF16)

    def wait_lat(e):
        copy(lat_in, lat_dst(e), LAT_Z + e - 1, LAT_Z + e - 1, sib).wait_recv()
        copy(kr.at[0], kr.at[e], ROPE_Z + e - 1, ROPE_Z + e - 1, sib).wait_recv()
        a = copy(lat_dst(e), lat_dst(4 + e), LAT_C + e, LAT_C + e, sib)
        b = copy(kr.at[e], kr.at[4 + e], ROPE_C + e, ROPE_C + e, sib)
        a.start()
        b.start()
        return [a, b]

    project(0)
    q_r.wait_recv()
    q_f.start()
    c_l.wait_recv()
    c_f.start()
    forwards = wait_lat(1) + wait_lat(3)
    q_l.wait_recv()
    project_3_ready = c_l
    project(3)
    c_r.wait_recv()
    project(1)
    forwards += wait_lat(2)
    lat_own.wait_recv()
    kr_own.wait_recv()
    for op in forwards:
        op.wait_recv()

    def key_block(b, carry):
        r16 = kr[b]
        wide = jnp.concatenate([r16.astype(F32), jnp.zeros((AUG - R - ROPE, TOK), F32)], axis=0)
        kaug[b, :, R:AUG] = jnp.transpose(wide).astype(BF16)
        lat_t[0:R, pl.ds(pl.multiple_of(b * TOK, TOK), TOK)] = jnp.transpose(kaug[b, :, 0:R])
        lat_t[R:R + ROPE, pl.ds(pl.multiple_of(b * TOK, TOK), TOK)] = r16
        return carry

    lax.fori_loop(0, NK, key_block, 0)

    key_order = []
    for cr in range(2):
        for e in range(4):
            cc = c if cr == 0 else 1 - c
            key_order.append(bo[(((zh + 4 - e) % 4) * 4 + x) * 2 + cc])

    ki, qi = iota((TOK, ROWS), 0), iota((TOK, ROWS), 1)
    lag = ki - qi % TOK

    def lanes(slot):
        return pl.ds(pl.multiple_of(slot * ROWS, ROWS), ROWS)

    def scores(slot):
        keys = kaug[...].reshape(KEYS, AUG)
        s_t[:, lanes(slot)] = nn(keys, qa_t[slot])
        q_order = bo[(zh * 4 + (x + 4 - slot) % 4) * 2 + c]
        top = jnp.full((8, ROWS), NEG, F32)
        for b in range(NK):
            rows = slice(b * TOK, (b + 1) * TOK)
            allowed = lag <= (q_order - key_order[b]) * TOK
            v = jnp.where(allowed, s_t[rows, lanes(slot)] * (SCALE * LOG2E), NEG)
            s_t[rows, lanes(slot)] = v
            top = jnp.maximum(top, jnp.max(v.reshape(TOK // 8, 8, ROWS), axis=0))
        top = jnp.max(top, axis=0, keepdims=True)
        total = jnp.zeros((8, ROWS), F32)
        for b in range(NK):
            rows = slice(b * TOK, (b + 1) * TOK)
            e = jnp.exp2(s_t[rows, lanes(slot)] - top)
            total = total + jnp.sum(e.reshape(TOK // 8, 8, ROWS), axis=0)
        total = jnp.sum(total, axis=0, keepdims=True)
        return top + jnp.log2(total)

    lse[...] = jnp.zeros_like(lse)
    lse[0:1, :] = scores(0)
    lse[1:2, :] = scores(1)
    lse[3:4, :] = scores(3)
    q_f.wait_recv()
    c_f.wait_recv()
    project(2)
    lse[2:3, :] = scores(2)

    stats = [copy(lse, lse_r.at[d - 1], STAT + d - 1, STAT + d - 1, dev(z, x + d, y, c)) for d in range(1, 4)]
    for op in stats:
        op.start()

    d_r.wait_recv()
    d_l.wait_recv()
    d_o.wait_recv()

    def dots_step(slot, carry):
        keys = kaug[:, :, 0:R].reshape(KEYS, R)
        dots_t[:, lanes(slot)] = nn(keys, o_lat_t[slot]) - delta[slot, 0:1, :]
        return carry

    lax.fori_loop(0, NQ, dots_step, 0)
    for op in stats:
        op.wait_recv()
    for slot in range(NQ):
        parts = [lse[slot:slot + 1, :]]
        for d in range(1, 4):
            row = (slot - d) % 4
            parts.append(lse_r[d - 1, row:row + 1, :])
        top = jnp.maximum(jnp.maximum(parts[0], parts[1]), jnp.maximum(parts[2], parts[3]))
        total = sum(jnp.exp2(p - top) for p in parts)
        m_loc[slot] = jnp.broadcast_to(top + jnp.log2(total), (8, ROWS))

    def grad_step(slot, carry):
        log_total = m_loc[slot, 0:1, :]
        for b in range(NK):
            rows = slice(b * TOK, (b + 1) * TOK)
            w = jnp.exp2(s_t[rows, lanes(slot)] - log_total)
            pr_t[rows, lanes(slot)] = w.astype(BF16)
            gs_t[rows, lanes(slot)] = (w * dots_t[rows, lanes(slot)] * SCALE).astype(BF16)
        return carry

    lax.fori_loop(0, NQ, grad_step, 0)

    half = KEYS // 2

    def key_grad(rows):
        q = q_lat[...].reshape(NQ * ROWS, R)
        o = o_lat[...].reshape(NQ * ROWS, R)
        return nn(gs_t[rows, :], q) + nn(pr_t[rows, :], o)

    def rope_grad(rows):
        total = jnp.zeros((ROPE, half), F32)
        for slot in range(NQ):
            total = total + nt(qa_t[slot, R:R + ROPE, :], gs_t[rows, slot * ROWS:(slot + 1) * ROWS])
        return total

    hi_rows, lo_rows = slice(half, KEYS), slice(0, half)
    dl_send[...] = key_grad(hi_rows).astype(BF16)
    dl_c = copy(dl_send, dl_rcv, DL_C, DL_C, sib)
    dl_c.start()
    rg = rope_grad(hi_rows)
    for e in range(4):
        dr_send[e] = rg[:, e * TOK:(e + 1) * TOK]
    dr_cc = copy(dr_send, dr_c, DR_C, DR_C, sib)
    dr_cc.start()
    dl_own[...] = key_grad(lo_rows)
    rg = rope_grad(lo_rows)
    dl_c.wait_recv()
    for j in range(4):
        v = dl_own[:, j * 128:(j + 1) * 128] + dl_rcv[:, j * 128:(j + 1) * 128].astype(F32)
        y_f[j] = v
        y_send[j] = v.astype(BF16)
    dl_y = [copy(y_send.at[(y + d) % 4], y_rcv.at[d - 1], DL_Y + d - 1, DL_Y + d - 1, dev(z, x, y + d, c)) for d in range(1, 4)]
    for op in dl_y:
        op.start()
    dr_cc.wait_recv()
    for e in range(4):
        dr_f[e] = rg[:, e * TOK:(e + 1) * TOK] + dr_c[e]
    dr_zz = [copy(dr_f.at[e], dr_z.at[e - 1], DR_Z + e - 1, DR_Z + e - 1, dev(z + 8 - 2 * e, x, y, c)) for e in range(1, 4)]
    for op in dr_zz:
        op.start()

    dw_acc[...] = jnp.zeros_like(dw_acc)
    dqa[R + ROPE:AUG, :] = jnp.zeros((AUG - R - ROPE, ROWS), BF16)

    def query_grad(slot, keep):
        dqa[0:R + ROPE, :] = nn(lat_t[...], gs_t[:, lanes(slot)]).astype(BF16)
        for h in range(LH):
            cols = slice(h * HD, (h + 1) * HD)
            g = dqa[:, cols]
            dq = nn(waug_t[cols, :], g)
            if keep:
                dq_own[cols, :] = dq
            else:
                dq_send[slot, cols, :] = dq.astype(BF16)
            dw_acc[:, cols] += nn(g[0:R, :], q_all[slot, :, cols])

    dq_x = [copy(dq_send.at[d], dq_rcv.at[d - 1], DQ_X + d - 1, DQ_X + d - 1, dev(z, x + 4 - d, y, c)) for d in range(1, 4)]
    query_grad(2, False)
    dq_x[1].start()
    query_grad(1, False)
    dq_x[0].start()

    for op in dl_y:
        op.wait_recv()
    v = y_f[y]
    for d in range(3):
        v = v + y_rcv[d].astype(F32)
    for i in range(8):
        z_f[i] = v[i * 64:(i + 1) * 64, :]
        z_send[i] = v[i * 64:(i + 1) * 64, :].astype(BF16)
    dl_z = []
    dl_z_in = []
    for e in range(4):
        for t in range(2):
            if e == 0 and t == 1:
                continue
            tz = other if e == 0 else t
            k = e * 2 + t if e else 0
            dl_z.append(copy(
                z_send.at[e * 2 + tz], z_rcv.at[e * 2 + zl], DL_Z + k,
                DL_Z + (0 if e == 0 else e * 2 + zl), dev(2 * (zh + 4 - e) + tz, x, y, c)))
            if e:
                dl_z_in.append(copy(z_send.at[0], z_rcv.at[e * 2 + t], DL_Z + k, DL_Z + k, sib))
            else:
                dl_z_in.append(copy(z_send.at[0], z_rcv.at[other], DL_Z, DL_Z, sib))
    for op in dl_z:
        op.start()

    query_grad(3, False)
    dq_x[2].start()
    query_grad(0, True)

    for zz in range(4):
        for xx in range(4):
            for cc in range(2):
                r0 = ((zz * 4 + xx) * 2 + cc) * 16
                dw_f[cc, xx, zz] = dw_acc[r0:r0 + 16, :]
                dw_send[cc, xx, zz] = dw_acc[r0:r0 + 16, :].astype(BF16)
    dw_cc = copy(dw_send.at[1 - c], dw_c, DW_C, DW_C, sib)
    dw_cc.start()

    for op in dl_z_in:
        op.wait_recv()
    v = z_f[zl] + z_rcv[other].astype(F32)
    for i in range(2, 8):
        v = v + z_rcv[i].astype(F32)
    ag[head] = v

    def to_heads(buf, base):
        out, come = [], []
        for j in range(1, 8):
            to = (head + j) % 8
            src = (head + 8 - j) % 8
            target = dev(zh * 2 + to // 4, x, to % 4, c)
            out.append(copy(buf.at[head], buf.at[head], base + j, base + j, target))
            come.append(copy(buf.at[head], buf.at[src], base + j, base + j, target))
        for op in out:
            op.start()
        return out, come

    dl_out, dl_come = to_heads(ag, DL_G)

    for op in dr_zz:
        op.wait_recv()
    dr_g[head] = dr_f[0] + dr_z[0] + dr_z[1] + dr_z[2]
    dr_out, dr_come = to_heads(dr_g, DR_G)

    dw_cc.wait_recv()
    v = dw_f[c] + dw_c[...].astype(F32)
    dw_xf[...] = v
    dw_xs[...] = v.astype(BF16)
    dw_x = [copy(dw_xs.at[(x + d) % 4], dw_xr.at[d - 1], DW_X + d - 1, DW_X + d - 1, dev(z, x + d, y, c)) for d in range(1, 4)]
    for op in dw_x:
        op.start()

    for op in dq_x:
        op.wait_recv()
    v = dq_own[...]
    for d in range(3):
        v = v + dq_rcv[d].astype(F32)
    dq_out[...] = jnp.transpose(v).astype(BF16)

    for op in dw_x:
        op.wait_recv()
    v = dw_xf[x]
    for d in range(3):
        v = v + dw_xr[d].astype(F32)
    dw_zf[...] = v
    dw_zs[...] = v.astype(BF16)
    dw_z = [copy(dw_zs.at[(zh + d) % 4], dw_zr.at[d - 1], DW_Z + d - 1, DW_Z + d - 1, dev(z + 2 * d, x, y, c)) for d in range(1, 4)]
    for op in dw_z:
        op.start()

    for op in dl_come:
        op.wait_recv()
    for i in range(8):
        dlat_out[(i // 4) * 64:(i // 4) * 64 + 64, (i % 4) * 128:(i % 4) * 128 + 128] = ag[i]
    for op in dr_come:
        op.wait_recv()
    drope_out[...] = jnp.transpose(dr_g[...].reshape(KVG * ROPE, TOK))
    for op in dw_z:
        op.wait_recv()
    v = dw_zf[zh]
    for d in range(3):
        v = v + dw_zr[d].astype(F32)
    dw_out[...] = v

    sent = first + [q_f, c_f] + forwards + stats + [dl_c, dr_cc] + dl_y + dr_zz + dq_x
    sent += dl_z + [dw_cc] + dl_out + dr_out + dw_x + dw_z
    for op in sent:
        op.wait_send()


def on_device(block_order, queries, latent, rope_keys, w_uk, w_uv, cotangent, attn_out):
    vm = lambda shape, kind: pltpu.VMEM(shape, kind)
    scratch = [
        vm((NQ, TOK, LH * HD), BF16), vm((NQ, TOK, LH * HD), BF16), vm((NQ, 8, ROWS), F32),
        vm((NK, TOK, AUG), BF16), vm((NK, ROPE, TOK), BF16), vm((KVG * ROPE, TOK), BF16),
        vm((R + ROPE, KEYS), BF16), vm((AUG, LH * HD), BF16), vm((LH * HD, AUG), BF16),
        vm((NQ, AUG, ROWS), BF16), vm((NQ, ROWS, R), BF16), vm((NQ, R, ROWS), BF16), vm((NQ, ROWS, R), BF16),
        vm((KEYS, NQ * ROWS), F32), vm((KEYS, NQ * ROWS), F32),
        vm((KEYS, NQ * ROWS), BF16), vm((KEYS, NQ * ROWS), BF16),
        vm((8, ROWS), F32), vm((3, 8, ROWS), F32), vm((NQ, 8, ROWS), F32),
        vm((KEYS // 2, R), F32), vm((KEYS // 2, R), BF16), vm((KEYS // 2, R), BF16),
        vm((4, KEYS // 2, 128), F32), vm((4, KEYS // 2, 128), BF16), vm((3, KEYS // 2, 128), BF16),
        vm((8, 64, 128), F32), vm((8, 64, 128), BF16), vm((8, 64, 128), BF16), vm((8, 64, 128), F32),
        vm((AUG, ROWS), BF16), vm((NQ, LH * HD, TOK), BF16), vm((LH * HD, TOK), F32), vm((3, LH * HD, TOK), BF16),
        vm((R, LH * HD), F32), vm((2, 4, 4, 16, LH * HD), F32), vm((2, 4, 4, 16, LH * HD), BF16),
        vm((4, 4, 16, LH * HD), BF16), vm((4, 4, 16, LH * HD), F32), vm((4, 4, 16, LH * HD), BF16),
        vm((3, 4, 16, LH * HD), BF16), vm((4, 16, LH * HD), F32), vm((4, 16, LH * HD), BF16),
        vm((3, 16, LH * HD), BF16),
        vm((4, ROPE, TOK), F32), vm((4, ROPE, TOK), F32), vm((4, ROPE, TOK), F32),
        vm((3, ROPE, TOK), F32), vm((KVG, ROPE, TOK), F32),
        pltpu.SemaphoreType.DMA((N_COPY,)), pltpu.SemaphoreType.DMA((N_COPY,)),
    ]
    vmem = pl.BlockSpec(memory_space=pltpu.VMEM)
    dq, dlat, drope, dw = pl.pallas_call(
        kernel,
        out_shape=(
            jax.ShapeDtypeStruct((TOK, LH * HD), BF16),
            jax.ShapeDtypeStruct((TOK, R), F32),
            jax.ShapeDtypeStruct((TOK, KVG * ROPE), F32),
            jax.ShapeDtypeStruct((16, LH * HD), F32),
        ),
        in_specs=[pl.BlockSpec(memory_space=pltpu.SMEM)] + [vmem] * 7,
        out_specs=(vmem,) * 4,
        scratch_shapes=scratch,
        compiler_params=pltpu.CompilerParams(
            collective_id=0, has_side_effects=True, vmem_limit_bytes=60 * 1024 * 1024
        ),
        name="latent_attention_grad",
    )(block_order, queries, latent, rope_keys, w_uk, w_uv, cotangent, attn_out)
    dw = dw.reshape(16, LH, HD)[:, :, :NOPE].reshape(16, LH * NOPE)
    return dq, dlat, drope, dw


def solution(mesh):
    return jax.shard_map(
        on_device,
        mesh=mesh,
        in_specs=(
            P(),
            P("ctx", "head"),
            P("ctx", None),
            P("ctx", None),
            P(None, "head"),
            P(None, "head"),
            P("ctx", "head"),
            P("ctx", "head"),
        ),
        out_specs=(P("ctx", "head"), P("ctx", None), P("ctx", None), P("ctx", "head")),
        check_vma=False,
    )
```

```python
import math

import jax
import jax.numpy as jnp
from jax import lax
from jax.experimental import pallas as pl
from jax.experimental.pallas import tpu as pltpu
from jax.sharding import PartitionSpec as P

KVG = 8
NOPE = 112
ROPE = 16
HD = 128
TOK = 128
LH = 4
R = 512
AUG = 640
NQ = 4
ROWS = LH * TOK
F32 = jnp.float32
BF16 = jnp.bfloat16
NEG = -1e30
SCALE = 1.0 / math.sqrt(HD)
LOG2E = math.log2(math.e)
MESH = pl.DeviceIdType.MESH

PLACE = (0, 1, 3, 2)
STEP = (0, 1, 3, 2)

N_COPY = 0


def numbers(n):
    global N_COPY
    N_COPY += n
    return N_COPY - n


Q_R, Q_L, Q_F, C_R, C_L, C_F, D_R, D_L, D_F = (numbers(1) for _ in range(9))
LAT_Z, ROPE_Z, LAT_C, ROPE_C = numbers(4), numbers(4), numbers(3), numbers(4)
QUART_Z, QUART_Y, QUART_C = numbers(1), numbers(4), numbers(4)
STAT = numbers(4)
DL_C, DL_Y, DL_Z, DL_G = numbers(2), numbers(8), numbers(8), numbers(8)
DQ_X = numbers(4)
DW_C, DW_X, DW_Z = numbers(1), numbers(4), numbers(4)
DR_C, DR_Z, DR_G = numbers(1), numbers(4), numbers(8)


def nt(a, b):
    return lax.dot_general(a, b, (((1,), (1,)), ((), ())), preferred_element_type=F32)


def nn(a, b):
    return jnp.dot(a, b, preferred_element_type=F32)


def iota(shape, dim):
    return lax.broadcasted_iota(jnp.int32, shape, dim)


def kernel(
    bo, q_in, lat_in, rope_in, wuk_in, wuv_in, cot_in, att_in,
    dq_out, dlat_out, drope_out, dw_out,
    rope_v, wuk, wuv, att,
    q_all, c_all, delta, kaug, kr, rope_t, lat_t, waug, waug_t,
    qa_t, q_lat, o_lat_t, o_lat, s_t, dots_t, gs_t, pr_t,
    lse_p, lse, lse_r, log_tot,
    dl_send, dl_rcv, y_f, y_send, y_rcv, z_f, z_send, z_rcv, ag,
    dqa, dq_send, dq_own, dq_rcv,
    dw_acc, dw_f, dw_send, dw_c, dw_xf, dw_xs, dw_xr, dw_zf, dw_zs, dw_zr,
    dr_send, dr_c, dr_f, dr_z, dr_g,
    lsem, ssem, rsem,
):
    ctx = lax.axis_index("ctx")
    head = lax.axis_index("head")
    c, x, zh = ctx % 2, (ctx // 2) % 4, ctx // 8
    y, zl = head % 4, head // 4
    z = zh * 2 + zl
    other = 1 - zl

    def dev(zz, xx, yy, cc):
        zz, xx, yy = zz % 8, xx % 4, yy % 4
        return (((zz // 2) * 4 + xx) * 2 + cc, (zz % 2) * 4 + yy)

    sib = dev(z, x, y, 1 - c)

    def copy(src, dst, sid, rid, target):
        return pltpu.make_async_remote_copy(
            src_ref=src, dst_ref=dst, send_sem=ssem.at[sid], recv_sem=rsem.at[rid],
            device_id=target, device_id_type=MESH,
        )

    def start(*ops):
        for op in ops:
            op.start()
            sent.append(op)

    def arrive(*ops):
        for op in ops:
            op.wait_recv()

    sent = []

    barrier = pltpu.get_barrier_semaphore()
    peers = [dev(2 * zh + other, x, y + d, c) for d in range(1, 4)]
    peers += [dev(z + d, x, y, c) for d in (4, 3, 5, 2, 6, 1, 7)]
    peers += [dev(z, x, y + d, c) for d in range(1, 4)]
    peers += [dev(z, x + d, y, c) for d in range(1, 4)]
    peers += [sib]

    def lat_at(cr, place, rows=None):
        if rows is None:
            return kaug.at[cr, place, :, pl.ds(0, R)]
        return kaug.at[cr, place, rows, pl.ds(0, R)]

    loads = [
        pltpu.make_async_copy(rope_in, rope_v, lsem.at[0]),
        pltpu.make_async_copy(lat_in, lat_at(0, 0), lsem.at[1]),
        pltpu.make_async_copy(q_in, q_all.at[0], lsem.at[2]),
        pltpu.make_async_copy(cot_in, c_all.at[0], lsem.at[3]),
        pltpu.make_async_copy(wuk_in, wuk, lsem.at[4]),
        pltpu.make_async_copy(wuv_in, wuv, lsem.at[5]),
        pltpu.make_async_copy(att_in, att, lsem.at[6]),
    ]
    for op in loads:
        op.start()
    for p in peers:
        pl.semaphore_signal(barrier, inc=1, device_id=p, device_id_type=MESH)

    loads[0].wait()
    rope_t[...] = jnp.transpose(rope_v[...].astype(F32)).astype(BF16)
    kr[0, 0] = rope_t[pl.ds(pl.multiple_of(head * ROPE, ROPE), ROPE), :]
    for op in loads[1:]:
        op.wait()
    ones = jnp.ones((8, HD), BF16)
    for h in range(LH):
        cols = slice(h * HD, (h + 1) * HD)
        prod = c_all[0, :, cols].astype(F32) * att[:, cols].astype(F32)
        high = prod.astype(BF16)
        low = (prod - high.astype(F32)).astype(BF16)
        delta[0, :, h * TOK:(h + 1) * TOK] = nt(ones, high) + nt(ones, low)

    fi, fj = iota((LH * HD, LH * NOPE), 0), iota((LH * HD, LH * NOPE), 1)
    spread = ((fj == (fi // HD) * NOPE + fi % HD) & (fi % HD < NOPE)).astype(F32).astype(BF16)
    waug_t[:, 0:R] = nn(spread, wuk[...]).astype(BF16)
    ti, tj = iota((LH * HD, AUG - R), 0), iota((LH * HD, AUG - R), 1)
    waug_t[:, R:AUG] = (tj == ti % HD - NOPE).astype(F32).astype(BF16)
    waug[...] = jnp.transpose(waug_t[...])

    def project(slot):
        for h in range(LH):
            cols = slice(h * HD, (h + 1) * HD)
            rows = slice(h * TOK, (h + 1) * TOK)
            qh = q_all[slot, :, cols]
            ch = c_all[slot, :, cols]
            qa_t[slot, :, rows] = nt(waug[:, cols], qh).astype(BF16)
            q_lat[slot, rows, :] = nn(qh, waug_t[cols, 0:R]).astype(BF16)
            o_lat_t[slot, :, rows] = nt(wuv[:, cols], ch).astype(BF16)
            o_lat[slot, rows, :] = nt(ch, wuv[:, cols]).astype(BF16)

    def prepare(cr, place):
        r16 = kr[cr, place]
        wide = jnp.concatenate([r16.astype(F32), jnp.zeros((AUG - R - ROPE, TOK), F32)], axis=0)
        kaug[cr, place, :, R:AUG] = jnp.transpose(wide).astype(BF16)
        cols = slice((cr * 4 + place) * TOK, (cr * 4 + place + 1) * TOK)
        lat_t[0:R, cols] = jnp.transpose(kaug[cr, place, :, 0:R])
        lat_t[R:R + ROPE, cols] = r16

    prepare(0, 0)
    pl.semaphore_wait(barrier, len(peers))

    right, left = dev(z, x + 1, y, c), dev(z, x + 3, y, c)
    s = 2 * zl - 1
    to_1, to_2, to_3 = (dev(z + i * s + 8, x, y, c) for i in (1, 2, 3))
    near = 2 - zl
    early, late = 1 + zl, 2 - zl

    def rope_of(group):
        return rope_t.at[pl.ds(pl.multiple_of(group * ROPE, ROPE), ROPE), :]

    def quarter(yy):
        return pl.ds(pl.multiple_of(yy * 32, 32), 32)

    q_r = copy(q_all.at[0], q_all.at[1], Q_R, Q_R, right)
    q_l = copy(q_all.at[0], q_all.at[3], Q_L, Q_L, left)
    c_r = copy(c_all.at[0], c_all.at[1], C_R, C_R, right)
    c_l = copy(c_all.at[0], c_all.at[3], C_L, C_L, left)
    d_r = copy(delta.at[0], delta.at[1], D_R, D_R, right)
    d_l = copy(delta.at[0], delta.at[3], D_L, D_L, left)
    q_f = copy(q_all.at[1], q_all.at[2], Q_F, Q_F, right)
    c_f = copy(c_all.at[3], c_all.at[2], C_F, C_F, left)
    d_f = copy(delta.at[1], delta.at[2], D_F, D_F, right)
    part = quarter(y)
    quart = copy(lat_at(0, 0, part), lat_at(0, 3, part), QUART_Z, QUART_Z, to_3)
    lat_1 = copy(lat_at(0, 0), lat_at(0, near), LAT_Z + 1, LAT_Z + near, to_1)
    lat_2 = copy(lat_at(0, 0), lat_at(0, near), LAT_Z + 2, LAT_Z + near, to_2)
    rope_1 = copy(rope_of(other * 4 + y), kr.at[0, near], ROPE_Z + 1, ROPE_Z + near, to_1)
    rope_2 = copy(rope_of(head), kr.at[0, near], ROPE_Z + 2, ROPE_Z + near, to_2)
    rope_3 = copy(rope_of(other * 4 + y), kr.at[0, 3], ROPE_Z + 3, ROPE_Z + 3, to_3)
    lat_c = copy(lat_at(0, 0), lat_at(1, 0), LAT_C, LAT_C, sib)
    rope_c = [copy(kr.at[0, i], kr.at[1, i], ROPE_C + i, ROPE_C + i, sib) for i in (0, 3)]
    start(q_r, c_l, quart, lat_1, q_l, c_r, lat_2, lat_c, rope_c[0], rope_3, rope_1, rope_2, d_r, d_l)

    def from_z(place):
        arrive(copy(lat_at(0, 0), lat_at(0, place), LAT_Z + place, LAT_Z + place, sib))
        arrive(copy(kr.at[0, 0], kr.at[0, place], ROPE_Z + place, ROPE_Z + place, sib))

    def to_core(place):
        start(copy(lat_at(0, place), lat_at(1, place), LAT_C + place, LAT_C + place, sib))
        start(copy(kr.at[0, place], kr.at[1, place], ROPE_C + place, ROPE_C + place, sib))

    def from_core(place):
        arrive(copy(lat_at(0, 0), lat_at(1, place), LAT_C + place, LAT_C + place, sib))
        arrive(copy(kr.at[0, 0], kr.at[1, place], ROPE_C + place, ROPE_C + place, sib))

    key_order = []
    for cr in range(2):
        for place in range(4):
            cc = c if cr == 0 else 1 - c
            key_order.append(bo[(((zh + 4 - STEP[place]) % 4) * 4 + x) * 2 + cc])
    lag = iota((TOK, ROWS), 0) - iota((TOK, ROWS), 1) % TOK

    def lanes(slot):
        return pl.ds(pl.multiple_of(slot * ROWS, ROWS), ROWS)

    def keys_of(a, b, width):
        return kaug[:, a:b, :, 0:width].reshape(2 * (b - a) * TOK, width)

    def scores(slot, a, b):
        v = nn(keys_of(a, b, AUG), qa_t[slot])
        q_order = bo[(zh * 4 + (x + 4 - slot) % 4) * 2 + c]
        top = jnp.full((8, ROWS), NEG, F32)
        for cr in range(2):
            for place in range(a, b):
                i = cr * (b - a) + place - a
                allowed = lag <= (q_order - key_order[cr * 4 + place]) * TOK
                w = jnp.where(allowed, v[i * TOK:(i + 1) * TOK, :] * (SCALE * LOG2E), NEG)
                s_t[cr, place, :, lanes(slot)] = w
                top = jnp.maximum(top, jnp.max(w.reshape(TOK // 8, 8, ROWS), axis=0))
        top = jnp.max(top, axis=0, keepdims=True)
        total = jnp.zeros((8, ROWS), F32)
        for cr in range(2):
            for place in range(a, b):
                e = jnp.exp2(s_t[cr, place, :, lanes(slot)] - top)
                total = total + jnp.sum(e.reshape(TOK // 8, 8, ROWS), axis=0)
        return top + jnp.log2(jnp.sum(total, axis=0, keepdims=True))

    def dots(slot, a, b):
        v = nn(keys_of(a, b, R), o_lat_t[slot]) - delta[slot, 0:1, :]
        dots_t[:, a:b, :, lanes(slot)] = v.reshape(2, b - a, TOK, ROWS)

    def both_step(group, a, b):
        def step(i, carry):
            slot = i + i // 2
            lse_p[slot, group:group + 1, :] = scores(slot, a, b)
            dots(slot, a, b)
            return carry

        return step

    project(0)
    from_core(0)
    prepare(1, 0)
    both_step(0, 0, 1)(0, 0)
    arrive(q_r)
    start(q_f)
    arrive(c_l)
    start(c_f)
    arrive(quart)
    quart_y = [copy(lat_at(0, 3, part), lat_at(0, 3, part), QUART_Y + d, QUART_Y + d, dev(z, x, y + d, c)) for d in range(1, 4)]
    quart_c = [copy(lat_at(0, 3, quarter((y + 4 - d) % 4)), lat_at(1, 3, quarter((y + 4 - d) % 4)), QUART_C + d, QUART_C + d, sib) for d in range(4)]
    start(*quart_y)
    start(quart_c[0])
    from_z(early)
    to_core(early)
    arrive(q_l)
    project(3)
    arrive(c_r)
    project(1)
    arrive(d_r)
    start(d_f)
    arrive(d_l)
    from_z(late)
    to_core(late)
    lax.fori_loop(1, 3, both_step(0, 0, 1), 0)
    for d in range(1, 4):
        src = quarter((y + 4 - d) % 4)
        arrive(copy(lat_at(0, 3, part), lat_at(0, 3, src), QUART_Y + d, QUART_Y + d, sib))
        start(quart_c[d])
    arrive(copy(kr.at[0, 0], kr.at[0, 3], ROPE_Z + 3, ROPE_Z + 3, sib))
    start(rope_c[1])
    from_core(1)
    from_core(2)
    for place in (1, 2):
        prepare(0, place)
        prepare(1, place)
    lax.fori_loop(0, 3, both_step(1, 1, 3), 0)
    arrive(*quart_c)
    arrive(rope_c[1])
    prepare(0, 3)
    prepare(1, 3)

    def last_step(i, carry):
        slot = i + i // 2
        parts = [scores(slot, 3, 4), lse_p[slot, 0:1, :], lse_p[slot, 1:2, :]]
        top = jnp.maximum(jnp.maximum(parts[0], parts[1]), parts[2])
        lse_p[slot, 2:3, :] = top + jnp.log2(sum(jnp.exp2(p - top) for p in parts))
        return carry

    lax.fori_loop(0, 3, last_step, 0)
    arrive(q_f)
    arrive(c_f)
    project(2)
    lse[...] = jnp.zeros_like(lse)
    lse[2:3, :] = scores(2, 0, 4)
    for slot in (0, 1, 3):
        lse[slot:slot + 1, :] = lse_p[slot, 2:3, :]

    stats = [copy(lse, lse_r.at[d - 1], STAT + d, STAT + d, dev(z, x + d, y, c)) for d in range(1, 4)]
    start(*stats)
    arrive(d_f)

    def dots_step(i, carry):
        dots(i + i // 2, 3, 4)
        return carry

    lax.fori_loop(0, 3, dots_step, 0)
    dots(2, 0, 4)
    arrive(*stats)
    for slot in range(NQ):
        parts = [lse[slot:slot + 1, :]]
        for d in range(1, 4):
            row = (slot - d) % 4
            parts.append(lse_r[d - 1, row:row + 1, :])
        top = jnp.maximum(jnp.maximum(parts[0], parts[1]), jnp.maximum(parts[2], parts[3]))
        total = sum(jnp.exp2(p - top) for p in parts)
        log_tot[slot] = jnp.broadcast_to(top + jnp.log2(total), (8, ROWS))

    def grad_step(slot, carry):
        log_total = log_tot[slot, 0:1, :]
        for cr in range(2):
            for place in range(4):
                w = jnp.exp2(s_t[cr, place, :, lanes(slot)] - log_total)
                pr_t[cr, place, :, lanes(slot)] = w.astype(BF16)
                gs_t[cr, place, :, lanes(slot)] = (w * dots_t[cr, place, :, lanes(slot)] * SCALE).astype(BF16)
        return carry

    lax.fori_loop(0, NQ, grad_step, 0)

    def key_grad(cr, chunk):
        q = q_lat[...].reshape(NQ * ROWS, R)
        o = o_lat[...].reshape(NQ * ROWS, R)
        g = gs_t[cr, 2 * chunk:2 * chunk + 2].reshape(2 * TOK, NQ * ROWS)
        p = pr_t[cr, 2 * chunk:2 * chunk + 2].reshape(2 * TOK, NQ * ROWS)
        return nn(g, q) + nn(p, o)

    def rope_grad(cr):
        total = jnp.zeros((ROPE, 4 * TOK), F32)
        for slot in range(NQ):
            g = gs_t[cr, :, :, slot * ROWS:(slot + 1) * ROWS].reshape(4 * TOK, ROWS)
            total = total + nt(qa_t[slot, R:R + ROPE, :], g)
        return total

    dl_c = [copy(dl_send.at[k], dl_rcv.at[k], DL_C + k, DL_C + k, sib) for k in range(2)]
    dr_cc = copy(dr_send, dr_c, DR_C, DR_C, sib)
    dl_y = []
    for k in range(2):
        dl_send[k] = key_grad(1, k).astype(BF16)
        start(dl_c[k])
        if k == 0:
            rg = rope_grad(1)
            for e in range(4):
                dr_send[e] = rg[:, e * TOK:(e + 1) * TOK]
            start(dr_cc)
        mine = key_grad(0, k)
        arrive(dl_c[k])
        for j in range(4):
            v = mine[:, j * 128:(j + 1) * 128] + dl_rcv[k, :, j * 128:(j + 1) * 128].astype(F32)
            y_f[k, j] = v
            y_send[k, j] = v.astype(BF16)
        ops = [copy(y_send.at[k, (y + d) % 4], y_rcv.at[k, d - 1], DL_Y + 4 * k + d, DL_Y + 4 * k + d, dev(z, x, y + d, c)) for d in (2, 1, 3)]
        start(*ops)
        dl_y.append(ops)

    rg = rope_grad(0)
    arrive(dr_cc)
    for e in range(4):
        dr_f[e] = rg[:, e * TOK:(e + 1) * TOK] + dr_c[e]
    dr_zz = [copy(dr_f.at[i], dr_z.at[i - 1], DR_Z + i, DR_Z + i, dev(z + 8 - 2 * STEP[i], x, y, c)) for i in range(1, 4)]
    start(*dr_zz)

    dw_acc[...] = jnp.zeros_like(dw_acc)
    dqa[R + ROPE:AUG, :] = jnp.zeros((AUG - R - ROPE, ROWS), BF16)

    def query_grad(slot, keep):
        g_all = gs_t[:, :, :, slot * ROWS:(slot + 1) * ROWS].reshape(8 * TOK, ROWS)
        dqa[0:R + ROPE, :] = nn(lat_t[...], g_all).astype(BF16)
        for h in range(LH):
            cols = slice(h * HD, (h + 1) * HD)
            g = dqa[:, cols]
            dq = nn(waug_t[cols, :], g)
            if keep:
                dq_own[cols, :] = dq
            else:
                dq_send[slot, cols, :] = dq.astype(BF16)
            dw_acc[:, cols] += nn(g[0:R, :], q_all[slot, :, cols])

    dq_x = [copy(dq_send.at[d], dq_rcv.at[d - 1], DQ_X + d, DQ_X + d, dev(z, x + 4 - d, y, c)) for d in range(1, 4)]

    dl_z_in = []

    def along_z(k):
        arrive(*dl_y[k])
        v = y_f[k, y]
        for d in range(3):
            v = v + y_rcv[k, d].astype(F32)
        for i in range(4):
            piece = v[i * 64:(i + 1) * 64, :]
            z_send[4 * k + i] = piece.astype(BF16)
            if k == 0 and i < 2:
                z_f[i] = piece
        for place in (2 * k, 2 * k + 1):
            e = STEP[place]
            for t in range(2):
                if e == 0 and t == 1:
                    continue
                tz = other if e == 0 else t
                start(copy(
                    z_send.at[place * 2 + tz], z_rcv.at[place * 2 + zl], DL_Z + place * 2 + t,
                    DL_Z + (0 if e == 0 else place * 2 + zl), dev(2 * (zh + 4 - e) + tz, x, y, c)))
                if e:
                    dl_z_in.append(copy(z_send.at[0], z_rcv.at[place * 2 + t], DL_Z + place * 2 + t, DL_Z + place * 2 + t, sib))
                else:
                    dl_z_in.append(copy(z_send.at[0], z_rcv.at[other], DL_Z, DL_Z, sib))

    query_grad(2, False)
    start(dq_x[1])
    query_grad(1, False)
    start(dq_x[0])
    along_z(0)
    query_grad(3, False)
    start(dq_x[2])
    query_grad(0, True)

    for zz in range(4):
        for xx in range(4):
            for cc in range(2):
                r0 = ((zz * 4 + xx) * 2 + cc) * 16
                dw_f[cc, xx, zz] = dw_acc[r0:r0 + 16, :]
                dw_send[cc, xx, zz] = dw_acc[r0:r0 + 16, :].astype(BF16)
    dw_cc = copy(dw_send.at[1 - c], dw_c, DW_C, DW_C, sib)
    start(dw_cc)
    along_z(1)

    def to_heads(buf, base):
        come = []
        for j in (6, 2, 5, 7, 1, 3, 4):
            to = (head + j) % 8
            src = (head + 8 - j) % 8
            target = dev(zh * 2 + to // 4, x, to % 4, c)
            start(copy(buf.at[head], buf.at[head], base + j, base + j, target))
            come.append(copy(buf.at[head], buf.at[src], base + j, base + j, target))
        return come

    arrive(dw_cc)
    v = dw_f[c] + dw_c[...].astype(F32)
    dw_xf[...] = v
    dw_xs[...] = v.astype(BF16)
    dw_x = [copy(dw_xs.at[(x + d) % 4], dw_xr.at[d - 1], DW_X + d, DW_X + d, dev(z, x + d, y, c)) for d in range(1, 4)]
    start(dw_x[1], dw_x[0], dw_x[2])

    arrive(*dr_zz)
    dr_g[head] = dr_f[0] + dr_z[0] + dr_z[1] + dr_z[2]
    dr_come = to_heads(dr_g, DR_G)

    arrive(*dq_x)
    v = dq_own[...]
    for d in range(3):
        v = v + dq_rcv[d].astype(F32)
    dq_out[...] = jnp.transpose(v).astype(BF16)

    arrive(*dl_z_in)
    v = z_f[zl] + z_rcv[other].astype(F32)
    for i in range(2, 8):
        v = v + z_rcv[i].astype(F32)
    ag[head] = v.astype(BF16)
    dl_come = to_heads(ag, DL_G)

    arrive(*dw_x)
    v = dw_xf[x]
    for d in range(3):
        v = v + dw_xr[d].astype(F32)
    dw_zf[...] = v
    dw_zs[...] = v.astype(BF16)
    dw_z = [copy(dw_zs.at[(zh + d) % 4], dw_zr.at[d - 1], DW_Z + d, DW_Z + d, dev(z + 2 * d, x, y, c)) for d in range(1, 4)]
    start(dw_z[1], dw_z[0], dw_z[2])

    arrive(*dr_come)
    drope_out[...] = dr_g[...]
    arrive(*dl_come)
    dlat_out[...] = ag[...]
    arrive(*dw_z)
    v = dw_zf[zh]
    for d in range(3):
        v = v + dw_zr[d].astype(F32)
    dw_out[...] = v

    for op in sent:
        op.wait_send()


def finish(dq_in, ag, dr_g, dw_in, dq_out, dlat_out, drope_out, dw_out):
    dq_out[...] = dq_in[...]
    for i in range(8):
        dlat_out[(i // 4) * 64:(i // 4) * 64 + 64, (i % 4) * 128:(i % 4) * 128 + 128] = ag[i].astype(F32)
    drope_out[...] = jnp.transpose(dr_g[...].reshape(KVG * ROPE, TOK))
    dw_out[...] = jnp.concatenate([dw_in[:, h * HD:h * HD + NOPE] for h in range(LH)], axis=1)


def on_device(block_order, queries, latent, rope_keys, w_uk, w_uv, cotangent, attn_out):
    vm = lambda shape, kind: pltpu.VMEM(shape, kind)
    wide = LH * HD
    scratch = [
        vm((TOK, KVG * ROPE), BF16), vm((LH * NOPE, R), BF16), vm((R, wide), BF16), vm((TOK, wide), BF16),
        vm((NQ, TOK, wide), BF16), vm((NQ, TOK, wide), BF16), vm((NQ, 8, ROWS), F32),
        vm((2, 4, TOK, AUG), BF16), vm((2, 4, ROPE, TOK), BF16), vm((KVG * ROPE, TOK), BF16),
        vm((R + ROPE, 8 * TOK), BF16), vm((AUG, wide), BF16), vm((wide, AUG), BF16),
        vm((NQ, AUG, ROWS), BF16), vm((NQ, ROWS, R), BF16), vm((NQ, R, ROWS), BF16), vm((NQ, ROWS, R), BF16),
        vm((2, 4, TOK, NQ * ROWS), F32), vm((2, 4, TOK, NQ * ROWS), F32),
        vm((2, 4, TOK, NQ * ROWS), BF16), vm((2, 4, TOK, NQ * ROWS), BF16),
        vm((NQ, 8, ROWS), F32), vm((8, ROWS), F32), vm((3, 8, ROWS), F32), vm((NQ, 8, ROWS), F32),
        vm((2, 2 * TOK, R), BF16), vm((2, 2 * TOK, R), BF16),
        vm((2, 4, 2 * TOK, 128), F32), vm((2, 4, 2 * TOK, 128), BF16), vm((2, 3, 2 * TOK, 128), BF16),
        vm((2, 64, 128), F32), vm((8, 64, 128), BF16), vm((8, 64, 128), BF16), vm((8, 64, 128), BF16),
        vm((AUG, ROWS), BF16), vm((NQ, wide, TOK), BF16), vm((wide, TOK), F32), vm((3, wide, TOK), BF16),
        vm((R, wide), F32), vm((2, 4, 4, 16, wide), F32), vm((2, 4, 4, 16, wide), BF16),
        vm((4, 4, 16, wide), BF16), vm((4, 4, 16, wide), F32), vm((4, 4, 16, wide), BF16),
        vm((3, 4, 16, wide), BF16), vm((4, 16, wide), F32), vm((4, 16, wide), BF16),
        vm((3, 16, wide), BF16),
        vm((4, ROPE, TOK), F32), vm((4, ROPE, TOK), F32), vm((4, ROPE, TOK), F32),
        vm((3, ROPE, TOK), F32), vm((KVG, ROPE, TOK), F32),
        pltpu.SemaphoreType.DMA((7,)), pltpu.SemaphoreType.DMA((N_COPY,)), pltpu.SemaphoreType.DMA((N_COPY,)),
    ]
    vmem = pl.BlockSpec(memory_space=pltpu.VMEM)
    anywhere = pl.BlockSpec(memory_space=pl.ANY)
    parts = pl.pallas_call(
        kernel,
        out_shape=(
            jax.ShapeDtypeStruct((TOK, wide), BF16),
            jax.ShapeDtypeStruct((8, 64, 128), BF16),
            jax.ShapeDtypeStruct((KVG, ROPE, TOK), F32),
            jax.ShapeDtypeStruct((16, wide), F32),
        ),
        in_specs=[pl.BlockSpec(memory_space=pltpu.SMEM)] + [anywhere] * 7,
        out_specs=(vmem,) * 4,
        scratch_shapes=scratch,
        compiler_params=pltpu.CompilerParams(
            collective_id=0, has_side_effects=True, vmem_limit_bytes=60 * 1024 * 1024
        ),
        name="latent_attention_grad",
    )(block_order, queries, latent, rope_keys, w_uk.T, w_uv, cotangent, attn_out)
    return pl.pallas_call(
        finish,
        out_shape=(
            jax.ShapeDtypeStruct((TOK, wide), BF16),
            jax.ShapeDtypeStruct((TOK, R), F32),
            jax.ShapeDtypeStruct((TOK, KVG * ROPE), F32),
            jax.ShapeDtypeStruct((16, LH * NOPE), F32),
        ),
        in_specs=[vmem] * 4,
        out_specs=(vmem,) * 4,
        name="finish",
    )(*parts)


def solution(mesh):
    return jax.shard_map(
        on_device,
        mesh=mesh,
        in_specs=(
            P(),
            P("ctx", "head"),
            P("ctx", None),
            P("ctx", None),
            P(None, "head"),
            P(None, "head"),
            P("ctx", "head"),
            P("ctx", "head"),
        ),
        out_specs=(P("ctx", "head"), P("ctx", None), P("ctx", None), P("ctx", "head")),
        check_vma=False,
    )
```

```python
import math

import jax
import jax.numpy as jnp
from jax import lax
from jax.experimental import pallas as pl
from jax.experimental.pallas import tpu as pltpu
from jax.sharding import PartitionSpec as P

KVG = 8
NOPE = 112
ROPE = 16
HD = 128
TOK = 128
LH = 4
R = 512
AUG = 640
NQ = 4
ROWS = LH * TOK
F32 = jnp.float32
BF16 = jnp.bfloat16
NEG = -1e30
SCALE = 1.0 / math.sqrt(HD)
LOG2E = math.log2(math.e)
MESH = pl.DeviceIdType.MESH

PLACE = (0, 1, 3, 2)
STEP = (0, 1, 3, 2)

N_COPY = 0


def numbers(n):
    global N_COPY
    N_COPY += n
    return N_COPY - n


Q_R, Q_L, C_R, C_L, D_R, D_L, D_F = (numbers(1) for _ in range(7))
Q_FR, Q_FL, C_FR, C_FL = (numbers(1) for _ in range(4))
LAT_Z, ROPE_Z, LAT_C, ROPE_C = numbers(4), numbers(4), numbers(3), numbers(4)
QUART_Z, QUART_Y, QUART_C = numbers(1), numbers(4), numbers(4)
STAT = numbers(4)
DL_C, DL_Y, DL_Z, DL_G = numbers(2), numbers(8), numbers(8), numbers(8)
DL_W, DL_FAR = numbers(8), numbers(1)
DQ_X = numbers(4)
DW_C, DW_X, DW_Z = numbers(1), numbers(4), numbers(4)
DR_C, DR_Z, DR_G = numbers(1), numbers(4), numbers(8)


def nt(a, b):
    return lax.dot_general(a, b, (((1,), (1,)), ((), ())), preferred_element_type=F32)


def nn(a, b):
    return jnp.dot(a, b, preferred_element_type=F32)


def iota(shape, dim):
    return lax.broadcasted_iota(jnp.int32, shape, dim)


def kernel(
    bo, q_in, lat_in, rope_in, wuk_in, wuv_in, cot_in, att_in,
    dq_out, dlat_out, drope_out, dw_out,
    rope_v, wuk, wuv, att,
    q_all, c_all, delta, kaug, kr, rope_t, lat_t, waug, waug_t,
    qa_t, q_lat, o_lat_t, o_lat, s_t, dots_t, gs_t, pr_t,
    lse_p, lse, lse_r, log_tot,
    dl_send, dl_rcv, y_f, y_send, y_rcv, z_f, z_send, z_rcv, w_rcv, far_send, far_rcv, ag,
    dqa, dq_send, dq_own, dq_rcv,
    dw_f, dw_send, dw_c, dw_xf, dw_xs, dw_xr, dw_zf, dw_zs, dw_zr,
    dr_send, dr_c, dr_f, dr_z, dr_g,
    lsem, ssem, rsem,
):
    ctx = lax.axis_index("ctx")
    head = lax.axis_index("head")
    c, x, zh = ctx % 2, (ctx // 2) % 4, ctx // 8
    y, zl = head % 4, head // 4
    z = zh * 2 + zl
    other = 1 - zl

    def dev(zz, xx, yy, cc):
        zz, xx, yy = zz % 8, xx % 4, yy % 4
        return (((zz // 2) * 4 + xx) * 2 + cc, (zz % 2) * 4 + yy)

    sib = dev(z, x, y, 1 - c)

    def copy(src, dst, sid, rid, target):
        return pltpu.make_async_remote_copy(
            src_ref=src, dst_ref=dst, send_sem=ssem.at[sid], recv_sem=rsem.at[rid],
            device_id=target, device_id_type=MESH,
        )

    def start(*ops):
        for op in ops:
            op.start()
            sent.append(op)

    def arrive(*ops):
        for op in ops:
            op.wait_recv()

    sent = []

    barrier = pltpu.get_barrier_semaphore()
    peers = [dev(2 * zh + other, x, y + d, c) for d in range(1, 4)]
    peers += [dev(z + d, x, y, c) for d in (4, 3, 5, 2, 6, 1, 7)]
    peers += [dev(z, x, y + d, c) for d in range(1, 4)]
    peers += [dev(z, x + d, y, c) for d in range(1, 4)]
    peers += [sib]

    def lat_at(cr, place, rows=None):
        if rows is None:
            return kaug.at[cr, place, :, pl.ds(0, R)]
        return kaug.at[cr, place, rows, pl.ds(0, R)]

    loads = [
        pltpu.make_async_copy(rope_in, rope_v, lsem.at[0]),
        pltpu.make_async_copy(lat_in, lat_at(0, 0), lsem.at[1]),
        pltpu.make_async_copy(q_in, q_all.at[0], lsem.at[2]),
        pltpu.make_async_copy(cot_in, c_all.at[0], lsem.at[3]),
        pltpu.make_async_copy(wuk_in, wuk, lsem.at[4]),
        pltpu.make_async_copy(wuv_in, wuv, lsem.at[5]),
        pltpu.make_async_copy(att_in, att, lsem.at[6]),
    ]
    for op in loads:
        op.start()
    for p in peers:
        pl.semaphore_signal(barrier, inc=1, device_id=p, device_id_type=MESH)

    loads[0].wait()
    rope_t[...] = jnp.transpose(rope_v[...].astype(F32)).astype(BF16)
    kr[0, 0] = rope_t[pl.ds(pl.multiple_of(head * ROPE, ROPE), ROPE), :]
    for op in loads[1:]:
        op.wait()
    ones = jnp.ones((8, HD), BF16)
    for h in range(LH):
        cols = slice(h * HD, (h + 1) * HD)
        prod = c_all[0, :, cols].astype(F32) * att[:, cols].astype(F32)
        high = prod.astype(BF16)
        low = (prod - high.astype(F32)).astype(BF16)
        delta[0, :, h * TOK:(h + 1) * TOK] = nt(ones, high) + nt(ones, low)

    fi, fj = iota((LH * HD, LH * NOPE), 0), iota((LH * HD, LH * NOPE), 1)
    spread = ((fj == (fi // HD) * NOPE + fi % HD) & (fi % HD < NOPE)).astype(F32).astype(BF16)
    waug_t[:, 0:R] = nn(spread, wuk[...]).astype(BF16)
    ti, tj = iota((LH * HD, AUG - R), 0), iota((LH * HD, AUG - R), 1)
    waug_t[:, R:AUG] = (tj == ti % HD - NOPE).astype(F32).astype(BF16)
    waug[...] = jnp.transpose(waug_t[...])

    def project_scores(slot):
        for h in range(LH):
            cols = slice(h * HD, (h + 1) * HD)
            qa_t[slot, :, h * TOK:(h + 1) * TOK] = nt(waug[:, cols], q_all[slot, :, cols]).astype(BF16)

    def project_rest(slot):
        for h in range(LH):
            cols = slice(h * HD, (h + 1) * HD)
            rows = slice(h * TOK, (h + 1) * TOK)
            ch = c_all[slot, :, cols]
            o_lat_t[slot, :, rows] = nt(wuv[:, cols], ch).astype(BF16)
            o_lat[slot, rows, :] = nt(ch, wuv[:, cols]).astype(BF16)
            q_lat[slot, rows, :] = nn(q_all[slot, :, cols], waug_t[cols, 0:R]).astype(BF16)

    def prepare(cr, place):
        r16 = kr[cr, place]
        wide = jnp.concatenate([r16.astype(F32), jnp.zeros((AUG - R - ROPE, TOK), F32)], axis=0)
        kaug[cr, place, :, R:AUG] = jnp.transpose(wide).astype(BF16)
        cols = pl.ds(pl.multiple_of((cr * 4 + place) * TOK, TOK), TOK)
        lat_t[0:R, cols] = jnp.transpose(kaug[cr, place, :, 0:R])
        lat_t[R:R + ROPE, cols] = r16

    prepare(0, 0)
    pl.semaphore_wait(barrier, len(peers))

    right, left = dev(z, x + 1, y, c), dev(z, x + 3, y, c)
    s = 2 * zl - 1
    to_1, to_2, to_3 = (dev(z + i * s + 8, x, y, c) for i in (1, 2, 3))
    near = 2 - zl
    early, late = 1 + zl, 2 - zl

    def rope_of(group):
        return rope_t.at[pl.ds(pl.multiple_of(group * ROPE, ROPE), ROPE), :]

    def quarter(yy):
        return pl.ds(pl.multiple_of(yy * 32, 32), 32)

    q_r = copy(q_all.at[0], q_all.at[1], Q_R, Q_R, right)
    q_l = copy(q_all.at[0], q_all.at[3], Q_L, Q_L, left)
    c_r = copy(c_all.at[0], c_all.at[1], C_R, C_R, right)
    c_l = copy(c_all.at[0], c_all.at[3], C_L, C_L, left)
    d_r = copy(delta.at[0], delta.at[1], D_R, D_R, right)
    d_l = copy(delta.at[0], delta.at[3], D_L, D_L, left)
    lo, hi = pl.ds(0, 2 * HD), pl.ds(2 * HD, 2 * HD)
    q_fr = copy(q_all.at[1, :, lo], q_all.at[2, :, lo], Q_FR, Q_FR, right)
    q_fl = copy(q_all.at[3, :, hi], q_all.at[2, :, hi], Q_FL, Q_FL, left)
    c_fr = copy(c_all.at[1, :, lo], c_all.at[2, :, lo], C_FR, C_FR, right)
    c_fl = copy(c_all.at[3, :, hi], c_all.at[2, :, hi], C_FL, C_FL, left)
    d_f = copy(delta.at[1], delta.at[2], D_F, D_F, right)
    part = quarter(y)
    quart = copy(lat_at(0, 0, part), lat_at(0, 3, part), QUART_Z, QUART_Z, to_3)
    lat_1 = copy(lat_at(0, 0), lat_at(0, near), LAT_Z + 1, LAT_Z + near, to_1)
    lat_2 = copy(lat_at(0, 0), lat_at(0, near), LAT_Z + 2, LAT_Z + near, to_2)
    rope_1 = copy(rope_of(other * 4 + y), kr.at[0, near], ROPE_Z + 1, ROPE_Z + near, to_1)
    rope_2 = copy(rope_of(head), kr.at[0, near], ROPE_Z + 2, ROPE_Z + near, to_2)
    rope_3 = copy(rope_of(other * 4 + y), kr.at[0, 3], ROPE_Z + 3, ROPE_Z + 3, to_3)
    lat_c = copy(lat_at(0, 0), lat_at(1, 0), LAT_C, LAT_C, sib)
    rope_c = [copy(kr.at[0, i], kr.at[1, i], ROPE_C + i, ROPE_C + i, sib) for i in (0, 3)]
    start(q_r, q_l, quart, lat_1, lat_c, rope_c[0], lat_2, c_r, c_l, rope_1, rope_3, rope_2, d_r, d_l)

    def from_z(place):
        arrive(copy(lat_at(0, 0), lat_at(0, place), LAT_Z + place, LAT_Z + place, sib))
        arrive(copy(kr.at[0, 0], kr.at[0, place], ROPE_Z + place, ROPE_Z + place, sib))

    def to_core(place):
        start(copy(lat_at(0, place), lat_at(1, place), LAT_C + place, LAT_C + place, sib))
        start(copy(kr.at[0, place], kr.at[1, place], ROPE_C + place, ROPE_C + place, sib))

    def from_core(place):
        arrive(copy(lat_at(0, 0), lat_at(1, place), LAT_C + place, LAT_C + place, sib))
        arrive(copy(kr.at[0, 0], kr.at[1, place], ROPE_C + place, ROPE_C + place, sib))

    def key_order(cr, place):
        step = place + (place // 2) * (1 - 2 * (place % 2))
        cc = c + cr - 2 * c * cr
        return bo[(((zh + 4 - step) % 4) * 4 + x) * 2 + cc]

    lag = iota((TOK, ROWS), 0) - iota((TOK, ROWS), 1) % TOK

    def lanes(slot):
        return pl.ds(pl.multiple_of(slot * ROWS, ROWS), ROWS)

    def scores(slot, place):
        v = nn(kaug[:, place].reshape(2 * TOK, AUG), qa_t[slot])
        q_order = bo[(zh * 4 + (x + 4 - slot) % 4) * 2 + c]
        top = jnp.full((8, ROWS), NEG, F32)
        tiles = []
        for cr in range(2):
            allowed = lag <= (q_order - key_order(cr, place)) * TOK
            w = jnp.where(allowed, v[cr * TOK:(cr + 1) * TOK, :] * (SCALE * LOG2E), NEG)
            s_t[cr, place, :, lanes(slot)] = w
            tiles.append(w)
            top = jnp.maximum(top, jnp.max(w.reshape(TOK // 8, 8, ROWS), axis=0))
        top = jnp.max(top, axis=0, keepdims=True)
        total = jnp.zeros((8, ROWS), F32)
        for w in tiles:
            e = jnp.exp2(w - top)
            total = total + jnp.sum(e.reshape(TOK // 8, 8, ROWS), axis=0)
        part = top + jnp.log2(jnp.sum(total, axis=0, keepdims=True))
        lse_p[place, slot] = jnp.broadcast_to(part, (8, ROWS))

    def loop(n, slot_of, place):
        def step(i, carry):
            scores(slot_of(i), place)
            return carry

        lax.fori_loop(0, n, step, 0)

    def odd(i):
        return 1 + 2 * i

    project_scores(0)
    project_rest(0)
    from_core(0)
    prepare(1, 0)
    scores(0, 0)
    arrive(q_r)
    start(q_fr)
    arrive(q_l)
    start(q_fl)
    arrive(quart)
    quart_y = [copy(lat_at(0, 3, part), lat_at(0, 3, part), QUART_Y + d, QUART_Y + d, dev(z, x, y + d, c)) for d in range(1, 4)]
    quart_c = [copy(lat_at(0, 3, quarter((y + 4 - d) % 4)), lat_at(1, 3, quarter((y + 4 - d) % 4)), QUART_C + d, QUART_C + d, sib) for d in range(4)]
    start(*quart_y)
    start(quart_c[0])
    from_z(early)
    to_core(early)
    project_scores(1)
    project_scores(3)
    prepare(0, early)
    loop(2, odd, 0)
    arrive(c_r)
    start(c_fr)
    arrive(c_l)
    start(c_fl)
    arrive(d_r)
    start(d_f)
    from_core(early)
    prepare(1, early)
    scores(0, early)
    from_z(late)
    to_core(late)
    loop(2, odd, early)
    for d in range(1, 4):
        src = quarter((y + 4 - d) % 4)
        arrive(copy(lat_at(0, 3, part), lat_at(0, 3, src), QUART_Y + d, QUART_Y + d, sib))
        start(quart_c[d])
    arrive(copy(kr.at[0, 0], kr.at[0, 3], ROPE_Z + 3, ROPE_Z + 3, sib))
    start(rope_c[1])
    arrive(q_fr, q_fl)
    project_scores(2)
    prepare(0, late)
    prepare(0, 3)
    scores(2, 0)
    scores(2, early)
    from_core(late)
    prepare(1, late)
    loop(4, lambda i: i, late)
    arrive(*quart_c)
    arrive(rope_c[1])
    prepare(1, 3)
    loop(4, lambda i: i, 3)

    def join(parts):
        top = jnp.maximum(jnp.maximum(parts[0], parts[1]), jnp.maximum(parts[2], parts[3]))
        return top + jnp.log2(sum(jnp.exp2(p - top) for p in parts))

    lse[...] = jnp.zeros_like(lse)
    for slot in range(NQ):
        lse[slot:slot + 1, :] = join([lse_p[place, slot, 0:1, :] for place in range(4)])

    stats = [copy(lse, lse_r.at[d - 1], STAT + d, STAT + d, dev(z, x + d, y, c)) for d in range(1, 4)]
    start(stats[1], stats[0], stats[2])
    project_rest(1)
    project_rest(3)
    arrive(d_l, d_f, c_fr, c_fl)
    project_rest(2)

    def dots_step(slot, carry):
        v = nn(kaug[:, :, :, 0:R].reshape(8 * TOK, R), o_lat_t[slot]) - delta[slot, 0:1, :]
        dots_t[:, :, :, lanes(slot)] = v.reshape(2, 4, TOK, ROWS)
        return carry

    lax.fori_loop(0, NQ, dots_step, 0)
    arrive(*stats)
    for slot in range(NQ):
        parts = [lse[slot:slot + 1, :]]
        for d in range(1, 4):
            row = (slot - d) % 4
            parts.append(lse_r[d - 1, row:row + 1, :])
        log_tot[slot] = jnp.broadcast_to(join(parts), (8, ROWS))

    def grad_step(slot, carry):
        log_total = log_tot[slot, 0:1, :]
        for cr in range(2):
            for place in range(4):
                w = jnp.exp2(s_t[cr, place, :, lanes(slot)] - log_total)
                pr_t[cr, place, :, lanes(slot)] = w.astype(BF16)
                gs_t[cr, place, :, lanes(slot)] = (w * dots_t[cr, place, :, lanes(slot)] * SCALE).astype(BF16)
        return carry

    lax.fori_loop(0, NQ, grad_step, 0)

    def key_grad(cr, chunk):
        q = q_lat[...].reshape(NQ * ROWS, R)
        o = o_lat[...].reshape(NQ * ROWS, R)
        g = gs_t[cr, 2 * chunk:2 * chunk + 2].reshape(2 * TOK, NQ * ROWS)
        p = pr_t[cr, 2 * chunk:2 * chunk + 2].reshape(2 * TOK, NQ * ROWS)
        return nn(g, q) + nn(p, o)

    def rope_grad(cr):
        total = jnp.zeros((ROPE, 4 * TOK), F32)
        for slot in range(NQ):
            g = gs_t[cr, :, :, slot * ROWS:(slot + 1) * ROWS].reshape(4 * TOK, ROWS)
            total = total + nt(qa_t[slot, R:R + ROPE, :], g)
        return total

    dl_c = [copy(dl_send.at[k], dl_rcv.at[k], DL_C + k, DL_C + k, sib) for k in range(2)]
    dr_cc = copy(dr_send, dr_c, DR_C, DR_C, sib)
    dl_y = []
    dl_w_in = []
    far_y = (y + 2) % 4

    def to_owners(k, piece, landing, base):
        come = []
        for place in (2 * k, 2 * k + 1):
            e = STEP[place]
            for t in range(2):
                if e == 0 and t == 1:
                    continue
                tz = other if e == 0 else t
                i = (place % 2) * 2
                start(copy(
                    piece(i + tz), landing.at[place * 2 + zl], base + place * 2 + t,
                    base + (0 if e == 0 else place * 2 + zl), dev(2 * (zh + 4 - e) + tz, x, y, c)))
                at = base + place * 2 + t
                come.append(copy(z_send.at[0], landing.at[place * 2 + t if e else other], at, at, sib))
        return come

    for k in range(2):
        dl_send[k] = key_grad(1, k).astype(BF16)
        start(dl_c[k])
        mine = key_grad(0, k)
        if k == 1:
            rg = rope_grad(1)
            for e in range(4):
                dr_send[e] = rg[:, e * TOK:(e + 1) * TOK]
            start(dr_cc)
        arrive(dl_c[k])
        for j in range(4):
            v = mine[:, j * 128:(j + 1) * 128] + dl_rcv[k, :, j * 128:(j + 1) * 128].astype(F32)
            y_f[k, j] = v
            y_send[k, j] = v.astype(BF16)
        ops = [copy(y_send.at[k, (y + d) % 4], y_rcv.at[k, d // 2], DL_Y + 4 * k + d, DL_Y + 4 * k + d, dev(z, x, y + d, c)) for d in (1, 3)]
        start(*ops)
        dl_y.append(ops)
        dl_w_in.extend(to_owners(k, lambda i: y_send.at[k, far_y, pl.ds(i * 64, 64)], w_rcv, DL_W))

    for h in range(LH):
        dqa[h, R + ROPE:AUG, :] = jnp.zeros((AUG - R - ROPE, NQ * TOK), BF16)

    def latent_step(slot, carry):
        g = nn(lat_t[...], gs_t[:, :, :, lanes(slot)].reshape(8 * TOK, ROWS)).astype(BF16)
        for h in range(LH):
            dqa[h, 0:R + ROPE, pl.ds(pl.multiple_of(slot * TOK, TOK), TOK)] = g[:, h * TOK:(h + 1) * TOK]
        return carry

    dq_x = [copy(dq_send.at[d], dq_rcv.at[d - 1], DQ_X + d, DQ_X + d, dev(z, x + 4 - d, y, c)) for d in range(1, 4)]

    dl_z_in = []

    def along_z(k):
        arrive(*dl_y[k])
        v = y_f[k, y]
        for d in range(2):
            v = v + y_rcv[k, d].astype(F32)
        for i in range(4):
            piece = v[i * 64:(i + 1) * 64, :]
            z_send[4 * k + i] = piece.astype(BF16)
            if k == 0 and i < 2:
                z_f[i] = piece
        dl_z_in.extend(to_owners(k, lambda i: z_send.at[4 * k + i], z_rcv, DL_Z))

    lax.fori_loop(0, 3, latent_step, 0)
    along_z(0)
    lax.fori_loop(3, NQ, latent_step, 0)

    for h in range(LH):
        cols = slice(h * HD, (h + 1) * HD)
        v = nn(dqa[h, 0:R, :], q_all[:, :, cols].reshape(NQ * TOK, HD))
        for zz in range(4):
            for xx in range(4):
                for cc in range(2):
                    r0 = ((zz * 4 + xx) * 2 + cc) * 16
                    dw_f[cc, xx, zz, :, cols] = v[r0:r0 + 16, :]
                    dw_send[cc, xx, zz, :, cols] = v[r0:r0 + 16, :].astype(BF16)
    dw_cc = copy(dw_send.at[1 - c], dw_c, DW_C, DW_C, sib)
    start(dw_cc)
    for h in range(LH):
        cols = slice(h * HD, (h + 1) * HD)
        v = nn(waug_t[cols, :], dqa[h])
        dq_own[cols, :] = v[:, 0:TOK]
        for slot in range(1, NQ):
            dq_send[slot, cols, :] = v[:, slot * TOK:(slot + 1) * TOK].astype(BF16)
    along_z(1)
    arrive(dw_cc)
    v = dw_f[c] + dw_c[...].astype(F32)
    dw_xf[...] = v
    dw_xs[...] = v.astype(BF16)
    dw_x = [copy(dw_xs.at[(x + d) % 4], dw_xr.at[d - 1], DW_X + d, DW_X + d, dev(z, x + d, y, c)) for d in range(1, 4)]
    start(dw_x[1], dw_x[0], dw_x[2])
    start(dq_x[1], dq_x[0], dq_x[2])

    rg = rope_grad(0)
    arrive(dr_cc)
    for e in range(4):
        dr_f[e] = rg[:, e * TOK:(e + 1) * TOK] + dr_c[e]
    dr_zz = [copy(dr_f.at[i], dr_z.at[i - 1], DR_Z + i, DR_Z + i, dev(z + 8 - 2 * STEP[i], x, y, c)) for i in range(1, 4)]
    start(*dr_zz)

    arrive(*dl_w_in)
    v = y_f[0, far_y, pl.ds(pl.multiple_of(zl * 64, 64), 64), :] + w_rcv[other].astype(F32)
    for i in range(2, 8):
        v = v + w_rcv[i].astype(F32)
    far_send[...] = v.astype(BF16)
    far_copy = copy(far_send, far_rcv, DL_FAR, DL_FAR, dev(z, x, y + 2, c))
    start(far_copy)

    def to_heads(buf, base):
        come = []
        for j in (6, 2, 5, 7, 1, 3, 4):
            to = (head + j) % 8
            src = (head + 8 - j) % 8
            target = dev(zh * 2 + to // 4, x, to % 4, c)
            start(copy(buf.at[head], buf.at[head], base + j, base + j, target))
            come.append(copy(buf.at[head], buf.at[src], base + j, base + j, target))
        return come

    arrive(*dr_zz)
    dr_g[head] = dr_f[0] + dr_z[0] + dr_z[1] + dr_z[2]
    dr_come = to_heads(dr_g, DR_G)

    arrive(*dw_x)
    v = dw_xf[x]
    for d in range(3):
        v = v + dw_xr[d].astype(F32)
    dw_zf[...] = v
    dw_zs[...] = v.astype(BF16)
    dw_z = [copy(dw_zs.at[(zh + d) % 4], dw_zr.at[d - 1], DW_Z + d, DW_Z + d, dev(z + 2 * d, x, y, c)) for d in range(1, 4)]
    start(dw_z[1], dw_z[0], dw_z[2])

    arrive(*dl_z_in)
    arrive(far_copy)
    v = z_f[zl] + z_rcv[other].astype(F32) + far_rcv[...].astype(F32)
    for i in range(2, 8):
        v = v + z_rcv[i].astype(F32)
    ag[head] = v.astype(BF16)
    dl_come = to_heads(ag, DL_G)

    arrive(*dq_x)
    v = dq_own[...]
    for d in range(3):
        v = v + dq_rcv[d].astype(F32)
    dq_out[...] = jnp.transpose(v).astype(BF16)

    arrive(*dr_come)
    drope_out[...] = dr_g[...]
    arrive(*dl_come)
    dlat_out[...] = ag[...]
    arrive(*dw_z)
    v = dw_zf[zh]
    for d in range(3):
        v = v + dw_zr[d].astype(F32)
    dw_out[...] = v

    for op in sent:
        op.wait_send()


def finish(dq_in, ag, dr_g, dw_in, dq_out, dlat_out, drope_out, dw_out):
    dq_out[...] = dq_in[...]
    for i in range(8):
        dlat_out[(i // 4) * 64:(i // 4) * 64 + 64, (i % 4) * 128:(i % 4) * 128 + 128] = ag[i].astype(F32)
    drope_out[...] = jnp.transpose(dr_g[...].reshape(KVG * ROPE, TOK))
    dw_out[...] = jnp.concatenate([dw_in[:, h * HD:h * HD + NOPE] for h in range(LH)], axis=1)


def on_device(block_order, queries, latent, rope_keys, w_uk, w_uv, cotangent, attn_out):
    vm = lambda shape, kind: pltpu.VMEM(shape, kind)
    wide = LH * HD
    scratch = [
        vm((TOK, KVG * ROPE), BF16), vm((LH * NOPE, R), BF16), vm((R, wide), BF16), vm((TOK, wide), BF16),
        vm((NQ, TOK, wide), BF16), vm((NQ, TOK, wide), BF16), vm((NQ, 8, ROWS), F32),
        vm((2, 4, TOK, AUG), BF16), vm((2, 4, ROPE, TOK), BF16), vm((KVG * ROPE, TOK), BF16),
        vm((R + ROPE, 8 * TOK), BF16), vm((AUG, wide), BF16), vm((wide, AUG), BF16),
        vm((NQ, AUG, ROWS), BF16), vm((NQ, ROWS, R), BF16), vm((NQ, R, ROWS), BF16), vm((NQ, ROWS, R), BF16),
        vm((2, 4, TOK, NQ * ROWS), F32), vm((2, 4, TOK, NQ * ROWS), F32),
        vm((2, 4, TOK, NQ * ROWS), BF16), vm((2, 4, TOK, NQ * ROWS), BF16),
        vm((4, NQ, 8, ROWS), F32), vm((8, ROWS), F32), vm((3, 8, ROWS), F32), vm((NQ, 8, ROWS), F32),
        vm((2, 2 * TOK, R), BF16), vm((2, 2 * TOK, R), BF16),
        vm((2, 4, 2 * TOK, 128), F32), vm((2, 4, 2 * TOK, 128), BF16), vm((2, 3, 2 * TOK, 128), BF16),
        vm((2, 64, 128), F32), vm((8, 64, 128), BF16), vm((8, 64, 128), BF16), vm((8, 64, 128), BF16),
        vm((64, 128), BF16), vm((64, 128), BF16), vm((8, 64, 128), BF16),
        vm((LH, AUG, NQ * TOK), BF16), vm((NQ, wide, TOK), BF16), vm((wide, TOK), F32), vm((3, wide, TOK), BF16),
        vm((2, 4, 4, 16, wide), F32), vm((2, 4, 4, 16, wide), BF16),
        vm((4, 4, 16, wide), BF16), vm((4, 4, 16, wide), F32), vm((4, 4, 16, wide), BF16),
        vm((3, 4, 16, wide), BF16), vm((4, 16, wide), F32), vm((4, 16, wide), BF16),
        vm((3, 16, wide), BF16),
        vm((4, ROPE, TOK), F32), vm((4, ROPE, TOK), F32), vm((4, ROPE, TOK), F32),
        vm((3, ROPE, TOK), F32), vm((KVG, ROPE, TOK), F32),
        pltpu.SemaphoreType.DMA((7,)), pltpu.SemaphoreType.DMA((N_COPY,)), pltpu.SemaphoreType.DMA((N_COPY,)),
    ]
    vmem = pl.BlockSpec(memory_space=pltpu.VMEM)
    anywhere = pl.BlockSpec(memory_space=pl.ANY)
    parts = pl.pallas_call(
        kernel,
        out_shape=(
            jax.ShapeDtypeStruct((TOK, wide), BF16),
            jax.ShapeDtypeStruct((8, 64, 128), BF16),
            jax.ShapeDtypeStruct((KVG, ROPE, TOK), F32),
            jax.ShapeDtypeStruct((16, wide), F32),
        ),
        in_specs=[pl.BlockSpec(memory_space=pltpu.SMEM)] + [anywhere] * 7,
        out_specs=(vmem,) * 4,
        scratch_shapes=scratch,
        compiler_params=pltpu.CompilerParams(
            collective_id=0, has_side_effects=True, vmem_limit_bytes=60 * 1024 * 1024
        ),
        name="latent_attention_grad",
    )(block_order, queries, latent, rope_keys, w_uk.T, w_uv, cotangent, attn_out)
    return pl.pallas_call(
        finish,
        out_shape=(
            jax.ShapeDtypeStruct((TOK, wide), BF16),
            jax.ShapeDtypeStruct((TOK, R), F32),
            jax.ShapeDtypeStruct((TOK, KVG * ROPE), F32),
            jax.ShapeDtypeStruct((16, LH * NOPE), F32),
        ),
        in_specs=[vmem] * 4,
        out_specs=(vmem,) * 4,
        name="finish",
    )(*parts)


def solution(mesh):
    return jax.shard_map(
        on_device,
        mesh=mesh,
        in_specs=(
            P(),
            P("ctx", "head"),
            P("ctx", None),
            P("ctx", None),
            P(None, "head"),
            P(None, "head"),
            P("ctx", "head"),
            P("ctx", "head"),
        ),
        out_specs=(P("ctx", "head"), P("ctx", None), P("ctx", None), P("ctx", "head")),
        check_vma=False,
    )
```
